32 devices in a mesh: grp: 2 (over y), fac: 16 (over z, x, core).
Axes of the slice: x: 2, y: 2, z: 4, core: 2. Of those that a mesh axis runs over, the one named last changes fastest.
Arguments:
- lattice_gen: int32 [2, 4096], P(None, 'fac'), may hold values from 1 to 65535
- lattice_shift: int32 [2, 32, 4096], P(None, 'grp', 'fac'), parts along dimension 1, may hold values from 0 to 65535
- loading: bfloat16 [4096, 4096], P('fac'), as said below
- basis_proj: bfloat16 [4096, 256], P('fac'), may hold values from -0.09375 to 0.09375
- basis_bias: float32 [256], replicated, may hold values from -3 to 3
- trade_block: int32 [10240], P(('grp', 'fac')), parts along dimension 0, may hold values from 0 to 31
- trade_weights: float32 [10240, 8], P(('grp', 'fac')), parts along dimension 0, may hold values from -2 to 2
- trade_notional: float32 [10240], P(('grp', 'fac')), parts along dimension 0, may hold values from -2.4 to 2.4
- trade_strike: float32 [10240], P(('grp', 'fac')), parts along dimension 0, may hold values from 0.6 to 1.6
- trade_owner: int32 [10240, 1], P(('grp', 'fac')), parts along dimension 0, may hold values from 0 to 15; in each aligned block of 320 rows (0 to 319, 320 to 639, ...) at most 40 rows name the same one
- trade_slot: int32 [10240], P(('grp', 'fac')), parts along dimension 0, may hold values from 0 to 23
Outputs:
- fitted: float32 [2, 384, 2048], P(None, 'fac', 'grp'), parts along dimension 2
- exposure: float32 [384, 4], P('fac', 'grp'), parts along dimension 1
The draws below stay inside these ranges and needn't reach their ends.
There are 2 independent parts, one for each index of `grp`. The reference program is written for one: setup_inputs(seed, part) draws one part's arguments, and reference() takes and returns one part's arrays. A program takes and returns all parts, laid end to end along the dimension named above; an argument that names none is the same for every part. Nothing has to cross between parts.
Inputs may be any that keep to these rules, and one draw needn't show every extreme that they name: `trade_owner`: among the trades of one index of fac no owner is named by more than 40 trades, a bound that some block reaches. `loading`: zero above the diagonal, 0.5 on it.
All inputs are finite; a program needn't handle non-finite values.
Results may differ from the reference program's by a relative error of at most 0.003.
Values may be sent and summed in bfloat16 or wider, within the bound.
A program may use at most 64 MiB of HBM per device.

```python
import math
import jax
import jax.numpy as jnp
import numpy as np
from jax import lax

FACTORS = 4096
BASIS = 256
BLOCK = 8
LATTICE = 65536
REPLICAS = 16
POINTS = 64
TRADE_DEV = 320
NSET_DEV = 24
SCENARIOS = 1024
TRADES = 5120
NSETS = 384
CAPACITY = 40
N_FAC = 16


def draw_loading(key, part):
    key = jax.random.fold_in(key, 11)
    row_index = jnp.arange(FACTORS)[:, None].astype(jnp.float32)
    col_index = jnp.arange(FACTORS)[None, :].astype(jnp.float32)
    noise = jax.random.normal(key, (FACTORS, FACTORS), jnp.float32)
    below = (col_index < row_index).astype(jnp.float32)
    diagonal = (col_index == row_index).astype(jnp.float32)
    scale = jnp.sqrt(0.75 / (row_index + 1.0))
    return (below * noise * scale + 0.5 * diagonal).astype(jnp.bfloat16)


def pair_layout(key):
    key_order, key_spread = jax.random.split(key)
    shuffled = jax.random.permutation(key_order, BASIS).astype(jnp.int32)
    midpoint = BASIS // 2
    columns = jnp.arange(BASIS, dtype=jnp.int32)
    source = columns.at[shuffled[midpoint:]].set(shuffled[:midpoint])
    copied = source != columns
    spread = jnp.exp(jax.random.uniform(key_spread, (BASIS,), jnp.float32, math.log(0.1), math.log(0.45)))
    return (source, copied, spread)


def draw_basis_proj(key, part):
    source, copied, spread = pair_layout(key)
    key = jax.random.fold_in(key, 23)
    key_base, key_jitter = jax.random.split(key)
    base = jnp.clip(jax.random.normal(key_base, (FACTORS, BASIS), jnp.float32), -4.0, 4.0)
    jitter = jnp.clip(jax.random.normal(key_jitter, (FACTORS, BASIS), jnp.float32), -4.0, 4.0)
    keeping = jnp.sqrt(1.0 - spread * spread)
    partner = base[:, source] * keeping[None, :] + spread[None, :] * jitter
    weights = jnp.where(copied[None, :], partner, base) * 0.015625
    return weights.astype(jnp.bfloat16)


def draw_basis_bias(key, part):
    source, copied, spread = pair_layout(key)
    key = jax.random.fold_in(key, 29)
    key_base, key_jitter = jax.random.split(key)
    base = jnp.clip(0.8 * jax.random.normal(key_base, (BASIS,), jnp.float32), -2.4, 2.4)
    jitter = jnp.clip(jax.random.normal(key_jitter, (BASIS,), jnp.float32), -3.0, 3.0)
    partner = base[source] + 0.2 * spread * jitter
    offsets = jnp.clip(jnp.where(copied, partner, base), -3.0, 3.0)
    return offsets.astype(jnp.float32)


def set_ends(drawn, rng, smallest, top_value):
    dims = drawn.shape
    place = [jax.random.randint(jax.random.fold_in(rng, axis), (), 0, dims[axis]) for axis in range(len(dims))]
    drawn = drawn.at[tuple(place)].set(smallest)
    longest = dims.index(max(dims))
    place[longest] = (place[longest] + 1) % dims[longest]
    return drawn.at[tuple(place)].set(top_value)


def levels(key, shape, pieces, least, largest):
    loudness, own = 1.0, jax.random.fold_in(key, 6)
    for position, shards_of in pieces:
        heights = jnp.exp(jax.random.uniform(jax.random.fold_in(own, position), (shards_of,), jnp.float32, least / len(pieces), largest / len(pieces)))
        loudness = loudness * jnp.repeat(heights, shape[position] // shards_of).reshape([-1 if axis == position else 1 for axis in range(len(shape))])
    return loudness


def shared_out(key, own, number, rows, count, top, limit, slope):
    sequence = jax.random.permutation(key, count)
    heavy_load, ordinary = shares(count, rows * top, limit, slope, True), shares(count, rows * top, limit, slope, False)
    places = jnp.arange(count)

    def named(lengths, rotation):
        used = int((lengths > 0).sum())
        fixed = max(1, used // 4)
        moved = fixed + (places - fixed + rotation * (used - fixed)) % max(1, count - fixed)
        return jnp.zeros((count,), jnp.int32).at[sequence[jnp.where(places < fixed, places, moved)]].set(jnp.asarray(lengths, jnp.int32))

    lengths = jnp.where(number % 4 == 0, named(heavy_load, number // 4), named(ordinary, number - number // 4 - 1))
    mixed = jax.random.permutation(jax.random.fold_in(own, 3), count)
    source_of, taker = mixed[0:count // 2 * 2:2], mixed[1:count // 2 * 2:2]
    margin = jnp.minimum(lengths[source_of] - 1, limit - lengths[taker]) // 2
    margin = jnp.where((source_of == sequence[0]) | (taker == sequence[0]) | (lengths[taker] == 0), 0, jnp.maximum(margin, 0))
    moved = jax.random.randint(jax.random.fold_in(own, 4), (count // 2,), 0, 1 << 20) % (margin + 1)
    lengths = lengths.at[source_of].add(-moved).at[taker].add(moved)
    labels = jnp.searchsorted(jnp.cumsum(lengths), jnp.arange(rows * top), side="right").astype(jnp.int32)
    table = labels.reshape(top, rows).T
    table = table[jax.random.permutation(jax.random.fold_in(own, 1), rows)]
    rotation = jax.random.randint(jax.random.fold_in(own, 2), (rows, 1), 0, top)
    return jnp.take_along_axis(table, (jnp.arange(top)[None, :] + rotation) % top, axis=1)


def shares(count, total, bound, slope, full):
    weights = [(1 << 20) // math.isqrt(standing ** slope) + 1 for standing in range(1, count + 1)]
    largest = bound if full else min(bound, max(-(-total // count), total * weights[0] // sum(weights)))
    least = 1 if total - largest >= count - 1 else 0
    holding, surplus = [largest] + [least] * (count - 1), total - largest - least * (count - 1)
    while surplus > 0:
        free = [i for i in range(1, count) if holding[i] < largest] or [i for i in range(1, count) if holding[i] < bound]
        pool, remaining = sum([weights[i] for i in free]), surplus
        for i in free:
            addition = min(bound - holding[i], max(1, remaining * weights[i] // pool), surplus)
            holding[i] = holding[i] + addition
            surplus = surplus - addition
    return np.array(holding)


def centred(own_key, shape, width, bound, shards=(), held_as=jnp.bfloat16):
    entries = jax.random.normal(own_key, shape, jnp.float32) * width
    if len(shards) > 0:
        entries = levels(own_key, shape, shards, -0.22, 0.18) * entries
    return jnp.clip(entries, min=-bound, max=bound).astype(held_as)


def setup_inputs(seed: int = 0, part: int = 0) -> dict:
    keys = jax.random.split(jax.random.key(seed), 12)
    part_keys = jax.random.split(jax.random.fold_in(keys[11], part), 12)
    lattice_gen = set_ends(jax.random.randint(keys[0], (2, FACTORS), 1, LATTICE), jax.random.fold_in(keys[0], 1), 1, LATTICE - 1).astype(jnp.int32)
    lattice_shift = set_ends(jax.random.randint(part_keys[1], (2, REPLICAS, FACTORS), 0, LATTICE), jax.random.fold_in(part_keys[1], 1), 0, LATTICE - 1).astype(jnp.int32)
    loading = draw_loading(jax.random.fold_in(keys[11], 71), part)
    basis_proj = draw_basis_proj(jax.random.fold_in(keys[11], 71), part)
    basis_bias = draw_basis_bias(jax.random.fold_in(keys[11], 71), part)
    trade_block = set_ends(jax.random.randint(part_keys[5], (TRADES,), 0, FACTORS // N_FAC // BLOCK), jax.random.fold_in(part_keys[5], 1), 0, (FACTORS // N_FAC // BLOCK) - 1).astype(jnp.int32)
    trade_weights = centred(part_keys[6], (TRADES, BLOCK), 0.35, 2.0, ((0, 16),), jnp.float32)
    trade_notional = centred(part_keys[7], (TRADES,), 0.4, 2.4, ((0, 16),), jnp.float32)
    trade_strike = jnp.clip(jnp.exp(math.log(1.6) - 0.98082923 * jax.random.uniform(part_keys[8], (TRADES,), jnp.float32) ** levels(part_keys[8], (TRADES,), ((0, 16),), -0.2, 0.2)), 0.6, 1.6)
    trade_owner_keys = jax.random.split(jax.random.fold_in(part_keys[9], 1), TRADES // TRADE_DEV)
    trade_owner_turns = jax.random.permutation(jax.random.fold_in(part_keys[9], 3), TRADES // TRADE_DEV)
    trade_owner = jax.vmap(lambda own, number: shared_out(jax.random.fold_in(part_keys[9], 2), own, number, TRADE_DEV, N_FAC, 1, CAPACITY, 2))(trade_owner_keys, trade_owner_turns).reshape((TRADES, 1))
    trade_slot = set_ends(jax.random.randint(part_keys[10], (TRADES,), 0, NSET_DEV), jax.random.fold_in(part_keys[10], 1), 0, NSET_DEV - 1).astype(jnp.int32)
    return {"lattice_gen": lattice_gen, "lattice_shift": lattice_shift, "loading": loading, "basis_proj": basis_proj, "basis_bias": basis_bias, "trade_block": trade_block, "trade_weights": trade_weights, "trade_notional": trade_notional, "trade_strike": trade_strike, "trade_owner": trade_owner, "trade_slot": trade_slot}


drift_rate = 0.25
ridge_term = 0.01
keep_share = 0.8
new_share = 0.6
root_two = 1.4142135623730951

def lattice_normals(lattice_gen, lattice_shift):
    points = jnp.arange(POINTS, dtype=jnp.int32)
    offsets = jnp.transpose(lattice_shift, (0, 2, 1))
    index = (points[None, None, None, :] * lattice_gen[:, :, None, None] + offsets[:, :, :, None]) % LATTICE
    unit = (index.astype(jnp.float32) + 0.5) / LATTICE
    normal = root_two * lax.erf_inv(2.0 * unit - 1.0)
    return normal.reshape(lattice_gen.shape[0], lattice_gen.shape[1], REPLICAS * POINTS).astype(jnp.bfloat16)

def reference(lattice_gen, lattice_shift, loading, basis_proj, basis_bias, trade_block, trade_weights, trade_notional, trade_strike, trade_owner, trade_slot):
    high = lax.Precision.HIGHEST
    normals = lattice_normals(lattice_gen, lattice_shift)
    first = jnp.dot(loading.astype(jnp.float32), normals[0].astype(jnp.float32), preferred_element_type=jnp.float32)
    second = jnp.dot(loading.astype(jnp.float32), normals[1].astype(jnp.float32), preferred_element_type=jnp.float32)
    state = jnp.stack([first, keep_share * first + new_share * second]).astype(jnp.bfloat16)
    phi = jnp.stack([jnp.tanh(jnp.dot(state[step].T.astype(jnp.float32), basis_proj.astype(jnp.float32), preferred_element_type=jnp.float32) + basis_bias[None, :]) for step in range(2)])
    gram = jnp.einsum('tsk,tsl->tkl', phi, phi, precision=high) / SCENARIOS + ridge_term * jnp.eye(BASIS, dtype=jnp.float32)[None]
    state_rows = state[1].astype(jnp.float32)
    home = jnp.arange(TRADES, dtype=jnp.int32) // TRADE_DEV
    first_row = (home * (FACTORS // N_FAC) + trade_block * BLOCK).astype(jnp.int32)
    driver = jnp.zeros((TRADES, SCENARIOS), jnp.float32)
    for column in range(BLOCK):
        driver = driver + trade_weights[:, column:column + 1] * state_rows[first_row + column]
    value = (trade_notional[:, None] * (jnp.exp(drift_rate * driver) - trade_strike[:, None])).astype(jnp.bfloat16)
    sets = (trade_owner[:, 0] * NSET_DEV + trade_slot).astype(jnp.int32)
    netting = jax.ops.segment_sum(value.astype(jnp.float32), sets, num_segments=NSETS)
    rhs = jnp.einsum('tsk,ns->tkn', phi, netting, precision=high) / SCENARIOS
    factor = jnp.linalg.cholesky(gram)
    middle = lax.linalg.triangular_solve(factor, rhs, left_side=True, lower=True)
    coeffs = lax.linalg.triangular_solve(factor, middle, left_side=True, lower=True, transpose_a=True)
    fitted = jnp.einsum('tkn,tsk->tns', coeffs, phi, precision=high)
    exposure = jnp.mean(jnp.maximum(fitted, 0.0), axis=2).T
    return (fitted, exposure)
```

```python
import functools
import math

import jax
import jax.numpy as jnp
from jax import lax
from jax.experimental import pallas as pl
from jax.experimental.pallas import tpu as pltpu
from jax.sharding import PartitionSpec as P

BLOCK = 8
LATTICE = 65536
REPLICAS = 16
POINTS = 64
NSET_DEV = 24
SET_ROWS = 32
SHARE = 2
SCENARIOS = REPLICAS * POINTS
LOCAL = SCENARIOS // SHARE
LOCAL_REPLICAS = REPLICAS // SHARE
LINES = 1 + LOCAL_REPLICAS

drift_rate = 0.25
ridge_term = 0.01
keep_share = 0.8
new_share = 0.6

VMEM_LIMIT = 56 * 1024 * 1024
HIGH = lax.Precision.HIGHEST
MESH = pl.DeviceIdType.MESH

LOG_SCALE = -2.0 / (15.001 * math.log(2.0))
NORMAL_TERMS = (
    3.00101966e00,
    1.55010142e00,
    -2.74155082e-01,
    3.36067480e-02,
    4.31695681e-02,
    -5.08279578e-02,
    3.10899462e-02,
    -1.21453725e-03,
    -1.43043690e-02,
    4.24694167e-03,
    2.40633730e-03,
)

INVERSE_STEPS = 11


def greet(me, n):
    barrier = pltpu.get_barrier_semaphore()
    for step in range(1, n):
        pl.semaphore_signal(
            barrier, inc=1, device_id={"fac": lax.rem(me + step, n)}, device_id_type=MESH
        )
    pl.semaphore_wait(barrier, n - 1)


def remote(src, dst, send, recv, peer):
    return pltpu.make_async_remote_copy(
        src_ref=src,
        dst_ref=dst,
        send_sem=send,
        recv_sem=recv,
        device_id={"fac": peer},
        device_id_type=MESH,
    )


def share_kernel(n, lines, load, proj, trade, lines_out, load_out, proj_out, trade_out, sends, recvs, mate_sends, mate_recvs, own):
    me = lax.axis_index("fac")
    core = lax.rem(me, SHARE)
    mate = me + 1 - 2 * core
    greet(me, n)
    copies = []
    for step in range(1, n):
        peer = lax.rem(me + step, n)
        copies.append(
            remote(lines.at[lax.rem(peer, SHARE)], lines_out.at[me], sends.at[step], recvs.at[step], peer)
        )
    for index, (src, dst) in enumerate(((trade, trade_out), (proj, proj_out), (load, load_out))):
        copies.append(remote(src, dst, mate_sends.at[index], mate_recvs.at[index], mate))
    for copy in copies:
        copy.start()
    keep = pltpu.make_async_copy(lines.at[core], lines_out.at[me], own)
    keep.start()
    keep.wait()
    for copy in copies:
        copy.wait()


def share(lines, load, proj, trade, n):
    hbm = pl.BlockSpec(memory_space=pl.ANY)
    return pl.pallas_call(
        functools.partial(share_kernel, n),
        out_shape=(
            jax.ShapeDtypeStruct((n,) + lines.shape[1:], lines.dtype),
            jax.ShapeDtypeStruct(load.shape, load.dtype),
            jax.ShapeDtypeStruct(proj.shape, proj.dtype),
            jax.ShapeDtypeStruct(trade.shape, trade.dtype),
        ),
        in_specs=[hbm] * 4,
        out_specs=[hbm] * 4,
        scratch_shapes=[
            pltpu.SemaphoreType.DMA((n,)),
            pltpu.SemaphoreType.DMA((n,)),
            pltpu.SemaphoreType.DMA((3,)),
            pltpu.SemaphoreType.DMA((3,)),
            pltpu.SemaphoreType.DMA,
        ],
        compiler_params=pltpu.CompilerParams(collective_id=0, has_side_effects=True),
    )(lines, load, proj, trade)


def mix_kernel(lines, load_own, load_mate, proj_own, proj_mate, trade_own, trade_mate, args, net, normal, base, mixed):
    step = pl.program_id(0)
    width = lines.shape[1]
    rows = load_own.shape[0]
    tile = 16

    @pl.when(step == 0)
    def _():
        mixed[...] = jnp.zeros_like(mixed)

    for t in range(2):
        base[...] = lax.broadcasted_iota(jnp.int32, (POINTS, width), 0) * lines[t * LINES : t * LINES + 1, :]

        def replica(r, carry):
            shift = lines[pl.ds(t * LINES + 1 + r, 1), :]
            for part in range(POINTS // tile):
                index = (base[part * tile : (part + 1) * tile, :] + shift) & (LATTICE - 1)
                x = index.astype(jnp.float32) * (2.0 / LATTICE) + (1.0 / LATTICE - 1.0)
                power = jnp.log((1.0 - x) * (1.0 + x)) * LOG_SCALE - 1.0
                ratio = power * NORMAL_TERMS[-1] + NORMAL_TERMS[-2]
                for term in NORMAL_TERMS[-3::-1]:
                    ratio = ratio * power + term
                start = pl.multiple_of(t * LOCAL + r * POINTS + part * tile, tile)
                normal[pl.ds(start, tile), :] = (ratio * x).astype(jnp.bfloat16)
            return carry

        lax.fori_loop(0, LOCAL_REPLICAS, replica, 0)

    def multiply(m, carry):
        span = pl.ds(pl.multiple_of(m * 256, 256), 256)
        left = normal[span, :]
        for half, load in enumerate((load_own, load_mate)):
            mixed[half, span, :] += lax.dot_general(
                left, load[...], (((1,), (1,)), ((), ())), preferred_element_type=jnp.float32
            )
        return carry

    lax.fori_loop(0, 2 * LOCAL // 256, multiply, 0)

    @pl.when(step == pl.num_programs(0) - 1)
    def _():
        picks = []
        members = []
        n_rows = net.shape[0] * SET_ROWS
        for trade in (trade_own, trade_mate):
            weights = jnp.concatenate([trade[0:8, :]] * (rows // BLOCK), axis=0)
            home = lax.shift_right_logical(lax.broadcasted_iota(jnp.int32, weights.shape, 0), 3)
            pick = jnp.where(home == trade[8:9, :].astype(jnp.int32), weights, 0.0)
            parts = []
            for _ in range(3):
                part = pick.astype(jnp.bfloat16)
                parts.append(part)
                pick = pick - part.astype(jnp.float32)
            picks.append(parts)
            sets = trade[11:12, :].astype(jnp.int32)
            members.append(
                jnp.where(lax.broadcasted_iota(jnp.int32, (n_rows, sets.shape[1]), 0) == sets, 1.0, 0.0).astype(jnp.bfloat16)
            )
        chunk = 128
        for m in range(LOCAL // chunk):
            low = slice(m * chunk, (m + 1) * chunk)
            high = slice(LOCAL + m * chunk, LOCAL + (m + 1) * chunk)
            totals = [0.0, 0.0]
            sums = 0.0
            for half, (proj, trade) in enumerate(((proj_own, trade_own), (proj_mate, trade_mate))):
                first = mixed[half, low, :]
                second = mixed[half, high, :]
                state = [
                    first.astype(jnp.bfloat16),
                    (keep_share * first + new_share * second).astype(jnp.bfloat16),
                ]
                for t in range(2):
                    totals[t] = totals[t] + jnp.dot(state[t], proj[...], preferred_element_type=jnp.float32)
                driver = 0.0
                for part in picks[half]:
                    driver = driver + jnp.dot(state[1], part, preferred_element_type=jnp.float32)
                value = (trade[9:10, :] * (jnp.exp(drift_rate * driver) - trade[10:11, :])).astype(jnp.bfloat16)
                sums = sums + lax.dot_general(
                    members[half], value, (((1,), (1,)), ((), ())), preferred_element_type=jnp.float32
                )
            for t in range(2):
                args[t, low, :] = totals[t]
            net[:, :, low] = sums.astype(jnp.bfloat16).reshape(net.shape[0], SET_ROWS, chunk)


def mix(lines, load_own, load_mate, proj_own, proj_mate, trade_own, trade_mate, n):
    rows, factors = load_own.shape
    width = 512
    basis = proj_own.shape[1]
    fixed = lambda j: (0, 0)
    return pl.pallas_call(
        mix_kernel,
        grid=(factors // width,),
        out_shape=(
            jax.ShapeDtypeStruct((2, LOCAL, basis), jnp.float32),
            jax.ShapeDtypeStruct((n, SET_ROWS, LOCAL), jnp.bfloat16),
        ),
        in_specs=[
            pl.BlockSpec((lines.shape[0], width), lambda j: (0, j)),
            pl.BlockSpec((rows, width), lambda j: (0, j)),
            pl.BlockSpec((rows, width), lambda j: (0, j)),
            pl.BlockSpec(proj_own.shape, fixed),
            pl.BlockSpec(proj_own.shape, fixed),
            pl.BlockSpec(trade_own.shape, fixed),
            pl.BlockSpec(trade_own.shape, fixed),
        ],
        out_specs=(
            pl.BlockSpec((2, LOCAL, basis), lambda j: (0, 0, 0)),
            pl.BlockSpec((n, SET_ROWS, LOCAL), lambda j: (0, 0, 0)),
        ),
        scratch_shapes=[
            pltpu.VMEM((2 * LOCAL, width), jnp.bfloat16),
            pltpu.VMEM((POINTS, width), jnp.int32),
            pltpu.VMEM((2, 2 * LOCAL, rows), jnp.float32),
        ],
        compiler_params=pltpu.CompilerParams(vmem_limit_bytes=VMEM_LIMIT),
    )(lines, load_own, load_mate, proj_own, proj_mate, trade_own, trade_mate)


def reduce_kernel(n, args, bias, net, phi, net_out, args_in, arg_sends, arg_recvs, net_sends, net_recvs, phi_sends, phi_recvs, mate_sends, mate_recvs, own):
    me = lax.axis_index("fac")
    core = lax.rem(me, SHARE)
    pair = lax.div(me, SHARE)
    mate = me + 1 - 2 * core
    pairs = n // SHARE
    block = LOCAL // pairs
    greet(me, n)

    def part(index):
        return pl.ds(pl.multiple_of(index * block, 8), block)

    def place(index, side):
        return pl.ds(pl.multiple_of(side * LOCAL + index * block, 8), block)

    arg_copies = []
    for step in range(1, pairs):
        other = lax.rem(pair + step, pairs)
        arg_copies.append(
            remote(args.at[:, part(other), :], args_in.at[pair], arg_sends.at[step], arg_recvs.at[step], SHARE * other + core)
        )
    net_copies = []
    for step in range(1, n):
        peer = lax.rem(me + step, n)
        net_copies.append(remote(net.at[peer], net_out.at[me], net_sends.at[step], net_recvs.at[step], peer))
    for copy in arg_copies + net_copies:
        copy.start()
    keep = pltpu.make_async_copy(net.at[me], net_out.at[me], own)
    keep.start()
    total = args[:, part(pair), :] + bias[...][None]
    for copy in arg_copies:
        copy.wait_recv()
    for step in range(1, pairs):
        total = total + args_in[lax.rem(pair + step, pairs)]
    mine = place(pair, core)
    phi[:, mine, :] = jnp.tanh(total)
    phi_copies = []
    for step in range(1, pairs):
        other = lax.rem(pair + step, pairs)
        phi_copies.append(
            remote(phi.at[:, mine, :], phi.at[:, mine, :], phi_sends.at[step], phi_recvs.at[step], SHARE * other + core)
        )
    mate_copies = [remote(phi.at[:, mine, :], phi.at[:, mine, :], mate_sends.at[0], mate_recvs.at[0], mate)]
    for copy in phi_copies + mate_copies:
        copy.start()
    for step in range(1, pairs):
        phi_copies[step - 1].wait_recv()
        there = place(lax.rem(pair - step + pairs, pairs), core)
        forward = remote(phi.at[:, there, :], phi.at[:, there, :], mate_sends.at[step], mate_recvs.at[step], mate)
        forward.start()
        mate_copies.append(forward)
    keep.wait()
    for copy in net_copies:
        copy.wait_recv()
    for copy in mate_copies:
        copy.wait_recv()
    for copy in arg_copies + net_copies + phi_copies + mate_copies:
        copy.wait_send()


def reduce(args, bias, net):
    n = net.shape[0]
    pairs = n // SHARE
    block = LOCAL // pairs
    basis = args.shape[2]
    vmem = pl.BlockSpec(memory_space=pltpu.VMEM)
    sems = [pltpu.SemaphoreType.DMA((k,)) for k in (pairs, pairs, n, n, pairs, pairs, pairs, pairs)]
    return pl.pallas_call(
        functools.partial(reduce_kernel, n),
        out_shape=(
            jax.ShapeDtypeStruct((2, SCENARIOS, basis), jnp.float32),
            jax.ShapeDtypeStruct(net.shape, net.dtype),
        ),
        in_specs=[vmem] * 3,
        out_specs=(vmem, vmem),
        scratch_shapes=[pltpu.VMEM((pairs, 2, block, basis), jnp.float32)] + sems + [pltpu.SemaphoreType.DMA],
        compiler_params=pltpu.CompilerParams(collective_id=1, has_side_effects=True, vmem_limit_bytes=VMEM_LIMIT),
    )(args, bias, net)


def regress_kernel(phi, net, fitted, exposure):
    n = net.shape[0]
    basis = phi.shape[2]
    sides = []
    for core in range(SHARE):
        side = net[core].astype(jnp.float32)
        for pair in range(1, n // SHARE):
            side = side + net[SHARE * pair + core].astype(jnp.float32)
        sides.append(side)
    netting = jnp.concatenate(sides, axis=1)
    eye = jnp.where(
        lax.broadcasted_iota(jnp.int32, (basis, basis), 0) == lax.broadcasted_iota(jnp.int32, (basis, basis), 1),
        1.0,
        0.0,
    )
    dot = functools.partial(jnp.dot, precision=HIGH, preferred_element_type=jnp.float32)
    grams = []
    rhs = []
    for t in range(2):
        basis_values = phi[t]
        grams.append(
            lax.dot_general(
                basis_values, basis_values, (((0,), (0,)), ((), ())), precision=HIGH, preferred_element_type=jnp.float32
            )
            * (1.0 / SCENARIOS)
            + ridge_term * eye
        )
        rhs.append(dot(netting, basis_values) * (1.0 / SCENARIOS))
    least, most = ridge_term, basis + ridge_term
    spread = (most - least) / (most + least)
    inverses = [eye * (2.0 / (most + least))] * 2
    for _ in range(INVERSE_STEPS):
        scale = 2.0 / (2.0 - spread * spread)
        spread = spread * spread / (2.0 - spread * spread)
        products = [dot(grams[t], inverses[t]) for t in range(2)]
        inverses = [scale * (2.0 * inverses[t] - dot(inverses[t], products[t])) for t in range(2)]
    for t in range(2):
        coeffs = dot(rhs[t], inverses[t])
        coeffs = coeffs + dot(rhs[t] - dot(coeffs, grams[t]), inverses[t])
        values = lax.dot_general(
            coeffs, phi[t], (((1,), (1,)), ((), ())), precision=HIGH, preferred_element_type=jnp.float32
        )[:NSET_DEV]
        fitted[t] = values
        exposure[:, t : t + 1] = jnp.sum(jnp.maximum(values, 0.0), axis=1, keepdims=True) * (1.0 / SCENARIOS)


def regress(phi, net):
    vmem = pl.BlockSpec(memory_space=pltpu.VMEM)
    return pl.pallas_call(
        regress_kernel,
        out_shape=(
            jax.ShapeDtypeStruct((2, NSET_DEV, SCENARIOS), jnp.float32),
            jax.ShapeDtypeStruct((NSET_DEV, 2), jnp.float32),
        ),
        in_specs=[vmem] * 2,
        out_specs=(vmem, vmem),
        compiler_params=pltpu.CompilerParams(vmem_limit_bytes=VMEM_LIMIT),
    )(phi, net)


def local(
    lattice_gen,
    lattice_shift,
    loading,
    basis_proj,
    basis_bias,
    trade_block,
    trade_weights,
    trade_notional,
    trade_strike,
    trade_owner,
    trade_slot,
):
    n = lax.axis_size("fac")
    factors = loading.shape[1]
    lines = jnp.concatenate(
        [
            jnp.concatenate(
                [lattice_gen[:, None, :], lattice_shift[:, side * LOCAL_REPLICAS : (side + 1) * LOCAL_REPLICAS, :]], axis=1
            ).reshape(1, 2 * LINES, -1)
            for side in range(SHARE)
        ],
        axis=0,
    )
    sets = trade_owner[:, 0] * SET_ROWS + trade_slot
    extra = jnp.stack([trade_block.astype(jnp.float32), trade_notional, trade_strike, sets.astype(jnp.float32)])
    trade = jnp.concatenate([trade_weights.T, extra, jnp.zeros_like(extra)], axis=0)
    all_lines, load_mate, proj_mate, trade_mate = share(lines, loading, basis_proj, trade, n)
    all_lines = jnp.transpose(all_lines, (1, 0, 2)).reshape(2 * LINES, factors)
    args, net = mix(all_lines, loading, load_mate, basis_proj, proj_mate, trade, trade_mate, n)
    phi, net = reduce(args, basis_bias[None, :], net)
    return regress(phi, net)


def solution(mesh):
    return jax.shard_map(
        local,
        mesh=mesh,
        in_specs=(
            P(None, "fac"),
            P(None, "grp", "fac"),
            P("fac", None),
            P("fac", None),
            P(),
            P(("grp", "fac")),
            P(("grp", "fac"), None),
            P(("grp", "fac")),
            P(("grp", "fac")),
            P(("grp", "fac"), None),
            P(("grp", "fac")),
        ),
        out_specs=(P(None, "fac", "grp"), P("fac", "grp")),
        check_vma=False,
    )
```

```python
import functools
import math

import jax
import jax.numpy as jnp
from jax import lax
from jax.experimental import pallas as pl
from jax.experimental.pallas import tpu as pltpu
from jax.sharding import PartitionSpec as P

BLOCK = 8
LATTICE = 65536
REPLICAS = 16
POINTS = 64
NSET_DEV = 24
SHARE = 2
SCENARIOS = REPLICAS * POINTS
LOCAL = SCENARIOS // SHARE
LOCAL_REPLICAS = REPLICAS // SHARE
LINES = 1 + LOCAL_REPLICAS

drift_rate = 0.25
ridge_term = 0.01
keep_share = 0.8
new_share = 0.6

VMEM_LIMIT = 56 * 1024 * 1024
HIGH = lax.Precision.HIGHEST
MESH = pl.DeviceIdType.MESH

LOG_SCALE = -2.0 / (15.001 * math.log(2.0))
NORMAL_TERMS = (
    3.00101966e00,
    1.55010142e00,
    -2.74155082e-01,
    3.36067480e-02,
    4.31695681e-02,
    -5.08279578e-02,
    3.10899462e-02,
    -1.21453725e-03,
    -1.43043690e-02,
    4.24694167e-03,
    2.40633730e-03,
)

INVERSE_STEPS = 10

CODES = 32767.0
CHUNK = 128


def encode(values):
    return jnp.round(values).astype(jnp.int32).astype(jnp.int16)


def decode(codes):
    return codes.astype(jnp.int32).astype(jnp.float32)


def greet(me, n):
    barrier = pltpu.get_barrier_semaphore()
    for step in range(1, n):
        pl.semaphore_signal(
            barrier, inc=1, device_id={"fac": lax.rem(me + step, n)}, device_id_type=MESH
        )
    pl.semaphore_wait(barrier, n - 1)


def remote(src, dst, send, recv, peer):
    return pltpu.make_async_remote_copy(
        src_ref=src,
        dst_ref=dst,
        send_sem=send,
        recv_sem=recv,
        device_id={"fac": peer},
        device_id_type=MESH,
    )


def share_kernel(n, *refs):
    count = (len(refs) - 5) // 2
    lines, *mine = refs[:count]
    lines_out, *theirs = refs[count : 2 * count]
    sends, recvs, mate_sends, mate_recvs, own = refs[2 * count :]
    me = lax.axis_index("fac")
    core = lax.rem(me, SHARE)
    mate = me + 1 - 2 * core
    greet(me, n)
    copies = []
    for step in range(1, n):
        peer = lax.rem(me + step, n)
        copies.append(
            remote(lines.at[lax.rem(peer, SHARE)], lines_out.at[me], sends.at[step], recvs.at[step], peer)
        )
    for index, (src, dst) in enumerate(zip(mine, theirs)):
        copies.append(remote(src, dst, mate_sends.at[index], mate_recvs.at[index], mate))
    for copy in copies:
        copy.start()
    keep = pltpu.make_async_copy(lines.at[core], lines_out.at[me], own)
    keep.start()
    keep.wait()
    for copy in copies:
        copy.wait()


def share(lines, arrays, n):
    hbm = pl.BlockSpec(memory_space=pl.ANY)
    count = len(arrays)
    return pl.pallas_call(
        functools.partial(share_kernel, n),
        out_shape=[jax.ShapeDtypeStruct((n,) + lines.shape[1:], lines.dtype)]
        + [jax.ShapeDtypeStruct(array.shape, array.dtype) for array in arrays],
        in_specs=[hbm] * (count + 1),
        out_specs=[hbm] * (count + 1),
        scratch_shapes=[
            pltpu.SemaphoreType.DMA((n,)),
            pltpu.SemaphoreType.DMA((n,)),
            pltpu.SemaphoreType.DMA((count,)),
            pltpu.SemaphoreType.DMA((count,)),
            pltpu.SemaphoreType.DMA,
        ],
        compiler_params=pltpu.CompilerParams(collective_id=0, has_side_effects=True),
    )(lines, *arrays)


def mix_kernel(lines, *refs):
    own, mate = refs[:8], refs[8:16]
    codes, scale, net, normal, base, mixed, args = refs[16:]
    load_own, load_mate = own[-1], mate[-1]
    step = pl.program_id(0)
    width = lines.shape[1]
    rows = load_own.shape[0]
    tile = 16

    @pl.when(step == 0)
    def _():
        mixed[...] = jnp.zeros_like(mixed)

    for t in range(2):
        base[...] = lax.broadcasted_iota(jnp.int32, (POINTS, width), 0) * lines[t * LINES : t * LINES + 1, :]

        def replica(r, carry):
            shift = lines[pl.ds(t * LINES + 1 + r, 1), :]
            for part in range(POINTS // tile):
                index = (base[part * tile : (part + 1) * tile, :] + shift) & (LATTICE - 1)
                x = index.astype(jnp.float32) * (2.0 / LATTICE) + (1.0 / LATTICE - 1.0)
                power = jnp.log((1.0 - x) * (1.0 + x)) * LOG_SCALE - 1.0
                ratio = power * NORMAL_TERMS[-1] + NORMAL_TERMS[-2]
                for term in NORMAL_TERMS[-3::-1]:
                    ratio = ratio * power + term
                start = pl.multiple_of(t * LOCAL + r * POINTS + part * tile, tile)
                normal[pl.ds(start, tile), :] = (ratio * x).astype(jnp.bfloat16)
            return carry

        lax.fori_loop(0, LOCAL_REPLICAS, replica, 0)

    def multiply(m, carry):
        span = pl.ds(pl.multiple_of(m * 256, 256), 256)
        left = normal[span, :]
        for half, load in enumerate((load_own, load_mate)):
            mixed[half, span, :] += lax.dot_general(
                left, load[...], (((1,), (1,)), ((), ())), preferred_element_type=jnp.float32
            )
        return carry

    lax.fori_loop(0, 2 * LOCAL // 256, multiply, 0)

    @pl.when(step == pl.num_programs(0) - 1)
    def _():
        picks = []
        members = []
        n_rows = net.shape[0] * NSET_DEV
        for block, slot, owner, _, _, weight, _, _ in (own, mate):
            weights = jnp.concatenate([weight[...]] * (rows // BLOCK), axis=0)
            home = lax.shift_right_logical(lax.broadcasted_iota(jnp.int32, weights.shape, 0), 3)
            pick = jnp.where(home == block[...], weights, 0.0)
            parts = []
            for _ in range(3):
                part = pick.astype(jnp.bfloat16)
                parts.append(part)
                pick = pick - part.astype(jnp.float32)
            picks.append(parts)
            sets = owner[...] * NSET_DEV + slot[...]
            members.append(
                jnp.where(lax.broadcasted_iota(jnp.int32, (n_rows, sets.shape[1]), 0) == sets, 1.0, 0.0).astype(jnp.bfloat16)
            )
        chunk = CHUNK
        largest = 0.0
        sums_of = []
        for m in range(LOCAL // chunk):
            low = slice(m * chunk, (m + 1) * chunk)
            high = slice(LOCAL + m * chunk, LOCAL + (m + 1) * chunk)
            totals = [0.0, 0.0]
            sums = 0.0
            for half, (_, _, _, notional, strike, _, proj, _) in enumerate((own, mate)):
                first = mixed[half, low, :]
                second = mixed[half, high, :]
                state = [
                    first.astype(jnp.bfloat16),
                    (keep_share * first + new_share * second).astype(jnp.bfloat16),
                ]
                for t in range(2):
                    totals[t] = totals[t] + jnp.dot(state[t], proj[...], preferred_element_type=jnp.float32)
                driver = 0.0
                for part in picks[half]:
                    driver = driver + jnp.dot(state[1], part, preferred_element_type=jnp.float32)
                value = (notional[...] * (jnp.exp(drift_rate * driver) - strike[...])).astype(jnp.bfloat16)
                sums = sums + lax.dot_general(
                    members[half], value, (((1,), (1,)), ((), ())), preferred_element_type=jnp.float32
                )
            for t in range(2):
                args[t, low, :] = totals[t]
                largest = jnp.maximum(largest, jnp.max(jnp.abs(totals[t])))
            sums_of.append(sums.reshape(net.shape[0], NSET_DEV, chunk))
        net[...] = jnp.concatenate(sums_of, axis=1).astype(jnp.bfloat16)
        unit = jnp.full(scale.shape, jnp.maximum(largest, 1e-30) * (1.0 / CODES), jnp.float32)
        scale[...] = unit
        inverse = 1.0 / unit[:1, :1]
        span = codes.shape[1] // 2
        for pair in range(codes.shape[0]):
            piece = jnp.concatenate([args[t, pair * span : (pair + 1) * span, :] for t in range(2)], axis=0)
            codes[pair] = encode(piece * inverse)


def mix(lines, own, mate, n):
    rows, factors = own[-1].shape
    width = 512
    basis = own[-2].shape[1]
    pairs = n // SHARE
    codes_shape = (pairs, 2 * LOCAL // pairs, basis)
    net_shape = (n, NSET_DEV * LOCAL // CHUNK, CHUNK)
    loads = pl.BlockSpec((rows, width), lambda j: (0, j))
    side = [pl.BlockSpec(array.shape, lambda j: (0, 0)) for array in own[:-1]] + [loads]
    return pl.pallas_call(
        mix_kernel,
        grid=(factors // width,),
        out_shape=(
            jax.ShapeDtypeStruct(codes_shape, jnp.int16),
            jax.ShapeDtypeStruct((8, 128), jnp.float32),
            jax.ShapeDtypeStruct(net_shape, jnp.bfloat16),
        ),
        in_specs=[pl.BlockSpec((lines.shape[0], width), lambda j: (0, j))] + side + side,
        out_specs=(
            pl.BlockSpec(codes_shape, lambda j: (0, 0, 0)),
            pl.BlockSpec((8, 128), lambda j: (0, 0)),
            pl.BlockSpec(net_shape, lambda j: (0, 0, 0)),
        ),
        scratch_shapes=[
            pltpu.VMEM((2 * LOCAL, width), jnp.bfloat16),
            pltpu.VMEM((POINTS, width), jnp.int32),
            pltpu.VMEM((2, 2 * LOCAL, rows), jnp.float32),
            pltpu.VMEM((2, LOCAL, basis), jnp.float32),
        ],
        compiler_params=pltpu.CompilerParams(vmem_limit_bytes=VMEM_LIMIT),
    )(lines, *own, *mate)


def reduce_kernel(n, codes, scale, bias, net, phi, net_out, codes_in, scales_in, arg_sends, arg_recvs, scale_sends, scale_recvs, net_sends, net_recvs, phi_sends, phi_recvs, mate_sends, mate_recvs, own):
    me = lax.axis_index("fac")
    core = lax.rem(me, SHARE)
    pair = lax.div(me, SHARE)
    mate = me + 1 - 2 * core
    pairs = n // SHARE
    greet(me, n)

    arg_copies = []
    for step in range(1, pairs):
        other = lax.rem(pair + step, pairs)
        peer = SHARE * other + core
        arg_copies.append(remote(scale, scales_in.at[pair], scale_sends.at[step], scale_recvs.at[step], peer))
        arg_copies.append(remote(codes.at[other], codes_in.at[pair], arg_sends.at[step], arg_recvs.at[step], peer))
    net_copies = []
    for step in range(1, n):
        peer = lax.rem(me + step, n)
        net_copies.append(remote(net.at[peer], net_out.at[me], net_sends.at[step], net_recvs.at[step], peer))
    for copy in arg_copies + net_copies:
        copy.start()
    keep = pltpu.make_async_copy(net.at[me], net_out.at[me], own)
    keep.start()
    total = decode(codes[pair]) * scale[:1, :1] + bias[...]
    for copy in arg_copies:
        copy.wait_recv()
    for step in range(1, pairs):
        other = lax.rem(pair + step, pairs)
        total = total + decode(codes_in[other]) * scales_in[other][:1, :1]
    phi[me] = encode(jnp.tanh(total) * CODES)
    phi_copies = []
    for step in range(1, pairs):
        peer = SHARE * lax.rem(pair + step, pairs) + core
        phi_copies.append(remote(phi.at[me], phi.at[me], phi_sends.at[step], phi_recvs.at[step], peer))
    mate_copies = [remote(phi.at[me], phi.at[me], mate_sends.at[0], mate_recvs.at[0], mate)]
    for copy in phi_copies + mate_copies:
        copy.start()
    for step in range(1, pairs):
        phi_copies[step - 1].wait_recv()
        there = SHARE * lax.rem(pair - step + pairs, pairs) + core
        forward = remote(phi.at[there], phi.at[there], mate_sends.at[step], mate_recvs.at[step], mate)
        forward.start()
        mate_copies.append(forward)
    keep.wait()
    for copy in net_copies:
        copy.wait_recv()
    for copy in mate_copies:
        copy.wait_recv()
    for copy in arg_copies + net_copies + phi_copies + mate_copies:
        copy.wait_send()


def reduce(codes, scale, bias, net):
    n = net.shape[0]
    pairs = n // SHARE
    vmem = pl.BlockSpec(memory_space=pltpu.VMEM)
    sems = [pltpu.SemaphoreType.DMA((k,)) for k in (pairs, pairs, pairs, pairs, n, n, pairs, pairs, pairs, pairs)]
    return pl.pallas_call(
        functools.partial(reduce_kernel, n),
        out_shape=(
            jax.ShapeDtypeStruct((n,) + codes.shape[1:], codes.dtype),
            jax.ShapeDtypeStruct(net.shape, net.dtype),
        ),
        in_specs=[vmem] * 4,
        out_specs=(vmem, vmem),
        scratch_shapes=[pltpu.VMEM(codes.shape, codes.dtype), pltpu.VMEM((pairs, 8, 128), jnp.float32)]
        + sems
        + [pltpu.SemaphoreType.DMA],
        compiler_params=pltpu.CompilerParams(collective_id=1, has_side_effects=True, vmem_limit_bytes=VMEM_LIMIT),
    )(codes, scale, bias, net)


def regress_kernel(phi_codes, net, fitted, exposure, phi):
    n = net.shape[0]
    basis = phi.shape[2]
    span = phi_codes.shape[1] // 2
    for index in range(n):
        piece = decode(phi_codes[index]) * (1.0 / CODES)
        start = (index % SHARE) * LOCAL + (index // SHARE) * span
        for t in range(2):
            phi[t, start : start + span, :] = piece[t * span : (t + 1) * span]
    parts = []
    for core in range(SHARE):
        side = net[core].astype(jnp.float32)
        for pair in range(1, n // SHARE):
            side = side + net[SHARE * pair + core].astype(jnp.float32)
        parts += [side[m * NSET_DEV : (m + 1) * NSET_DEV] for m in range(LOCAL // CHUNK)]
    netting = jnp.concatenate(parts, axis=1)
    eye = jnp.where(
        lax.broadcasted_iota(jnp.int32, (basis, basis), 0) == lax.broadcasted_iota(jnp.int32, (basis, basis), 1),
        1.0,
        0.0,
    )
    dot = functools.partial(jnp.dot, precision=HIGH, preferred_element_type=jnp.float32)
    grams = []
    rhs = []
    for t in range(2):
        basis_values = phi[t]
        grams.append(
            lax.dot_general(
                basis_values, basis_values, (((0,), (0,)), ((), ())), precision=HIGH, preferred_element_type=jnp.float32
            )
            * (1.0 / SCENARIOS)
            + ridge_term * eye
        )
        rhs.append(dot(netting, basis_values) * (1.0 / SCENARIOS))
    least, most = ridge_term, basis + ridge_term
    spread = (most - least) / (most + least)
    inverses = [eye * (2.0 / (most + least))] * 2
    for _ in range(INVERSE_STEPS):
        scale = 2.0 / (2.0 - spread * spread)
        spread = spread * spread / (2.0 - spread * spread)
        products = [dot(grams[t], inverses[t]) for t in range(2)]
        inverses = [scale * (2.0 * inverses[t] - dot(inverses[t], products[t])) for t in range(2)]
    for t in range(2):
        coeffs = dot(rhs[t], inverses[t])
        coeffs = coeffs + dot(rhs[t] - dot(coeffs, grams[t]), inverses[t])
        values = lax.dot_general(
            coeffs, phi[t], (((1,), (1,)), ((), ())), precision=HIGH, preferred_element_type=jnp.float32
        )
        fitted[t] = values
        exposure[:, t : t + 1] = jnp.sum(jnp.maximum(values, 0.0), axis=1, keepdims=True) * (1.0 / SCENARIOS)


def regress(phi, net):
    vmem = pl.BlockSpec(memory_space=pltpu.VMEM)
    return pl.pallas_call(
        regress_kernel,
        out_shape=(
            jax.ShapeDtypeStruct((2, NSET_DEV, SCENARIOS), jnp.float32),
            jax.ShapeDtypeStruct((NSET_DEV, 2), jnp.float32),
        ),
        in_specs=[vmem] * 2,
        out_specs=(vmem, vmem),
        scratch_shapes=[pltpu.VMEM((2, SCENARIOS, phi.shape[2]), jnp.float32)],
        compiler_params=pltpu.CompilerParams(vmem_limit_bytes=VMEM_LIMIT),
    )(phi, net)


def local(
    lattice_gen,
    lattice_shift,
    loading,
    basis_proj,
    basis_bias,
    trade_block,
    trade_weights,
    trade_notional,
    trade_strike,
    trade_owner,
    trade_slot,
):
    n = lax.axis_size("fac")
    factors = loading.shape[1]
    lines = jnp.concatenate(
        [
            jnp.concatenate(
                [lattice_gen[:, None, :], lattice_shift[:, side * LOCAL_REPLICAS : (side + 1) * LOCAL_REPLICAS, :]], axis=1
            ).reshape(1, 2 * LINES, -1)
            for side in range(SHARE)
        ],
        axis=0,
    )
    trades = [array.reshape(1, -1) for array in (trade_block, trade_slot, trade_owner, trade_notional, trade_strike)]
    own = trades + [trade_weights.T, basis_proj, loading]
    all_lines, *mate = share(lines, own, n)
    all_lines = jnp.transpose(all_lines, (1, 0, 2)).reshape(2 * LINES, factors)
    codes, scale, net = mix(all_lines, own, mate, n)
    phi, net = reduce(codes, scale, basis_bias[None, :], net)
    return regress(phi, net)


def solution(mesh):
    return jax.shard_map(
        local,
        mesh=mesh,
        in_specs=(
            P(None, "fac"),
            P(None, "grp", "fac"),
            P("fac", None),
            P("fac", None),
            P(),
            P(("grp", "fac")),
            P(("grp", "fac"), None),
            P(("grp", "fac")),
            P(("grp", "fac")),
            P(("grp", "fac"), None),
            P(("grp", "fac")),
        ),
        out_specs=(P(None, "fac", "grp"), P("fac", "grp")),
        check_vma=False,
    )
```

```python
import functools
import math

import jax
import jax.numpy as jnp
from jax import lax
from jax.experimental import pallas as pl
from jax.experimental.pallas import tpu as pltpu
from jax.sharding import PartitionSpec as P

BLOCK = 8
LATTICE = 65536
REPLICAS = 16
POINTS = 64
NSET_DEV = 24
SHARE = 2
SCENARIOS = REPLICAS * POINTS
LOCAL = SCENARIOS // SHARE
LOCAL_REPLICAS = REPLICAS // SHARE

drift_rate = 0.25
ridge_term = 0.01
keep_share = 0.8
new_share = 0.6

VMEM_LIMIT = 56 * 1024 * 1024
HIGH = lax.Precision.HIGHEST
MESH = pl.DeviceIdType.MESH

LOG_SCALE = -2.0 / (15.001 * math.log(2.0))
NORMAL_TERMS = (
    3.00101966e00,
    1.55010142e00,
    -2.74155082e-01,
    3.36067480e-02,
    4.31695681e-02,
    -5.08279578e-02,
    3.10899462e-02,
    -1.21453725e-03,
    -1.43043690e-02,
    4.24694167e-03,
    2.40633730e-03,
)

INVERSE_STEPS = 10

CODES = 32767.0
CHUNK = 128


def encode(values):
    return jnp.round(values).astype(jnp.int32).astype(jnp.int16)


def decode(codes):
    return codes.astype(jnp.int32).astype(jnp.float32)


def greet(me, n):
    barrier = pltpu.get_barrier_semaphore()
    for step in range(1, n):
        pl.semaphore_signal(
            barrier, inc=1, device_id={"fac": lax.rem(me + step, n)}, device_id_type=MESH
        )
    pl.semaphore_wait(barrier, n - 1)


def remote(src, dst, send, recv, peer):
    return pltpu.make_async_remote_copy(
        src_ref=src,
        dst_ref=dst,
        send_sem=send,
        recv_sem=recv,
        device_id={"fac": peer},
        device_id_type=MESH,
    )


def share_kernel(n, *refs):
    count = (len(refs) - 5) // 2
    gen, shift, *mine = refs[:count]
    gen_out, shift_out, *theirs = refs[count : 2 * count]
    sends, recvs, mate_sends, mate_recvs, own = refs[2 * count :]
    me = lax.axis_index("fac")
    core = lax.rem(me, SHARE)
    mate = me + 1 - 2 * core
    width = gen.shape[1]
    if len(gen_out.shape) == 2:
        columns = pl.ds(pl.multiple_of(me * width, 128), width)
        gen_to, shift_to = gen_out.at[:, columns], shift_out.at[:, :, columns]
    else:
        gen_to, shift_to = gen_out.at[me], shift_out.at[me]

    def replicas(side):
        return shift.at[:, pl.ds(pl.multiple_of(side * LOCAL_REPLICAS, LOCAL_REPLICAS), LOCAL_REPLICAS), :]

    greet(me, n)
    copies = []
    for step in range(1, n):
        peer = lax.rem(me + step, n)
        copies.append(remote(gen, gen_to, sends.at[0, step], recvs.at[0, step], peer))
        copies.append(remote(replicas(lax.rem(peer, SHARE)), shift_to, sends.at[1, step], recvs.at[1, step], peer))
    for index, (src, dst) in enumerate(zip(mine, theirs)):
        copies.append(remote(src, dst, mate_sends.at[index], mate_recvs.at[index], mate))
    for copy in copies:
        copy.start()
    keeps = [
        pltpu.make_async_copy(gen, gen_to, own.at[0]),
        pltpu.make_async_copy(replicas(core), shift_to, own.at[1]),
    ]
    for keep in keeps:
        keep.start()
    for copy in keeps + copies:
        copy.wait()


def share(gen, shift, arrays, n):
    hbm = pl.BlockSpec(memory_space=pl.ANY)
    count = len(arrays)
    width = gen.shape[1]
    whole = width % 128 == 0
    if whole:
        shapes = [(2, n * width), (2, LOCAL_REPLICAS, n * width)]
    else:
        shapes = [(n, 2, width), (n, 2, LOCAL_REPLICAS, width)]
    all_gen, all_shift, *mate = pl.pallas_call(
        functools.partial(share_kernel, n),
        out_shape=[jax.ShapeDtypeStruct(shape, gen.dtype) for shape in shapes]
        + [jax.ShapeDtypeStruct(array.shape, array.dtype) for array in arrays],
        in_specs=[hbm] * (count + 2),
        out_specs=[hbm] * (count + 2),
        scratch_shapes=[
            pltpu.SemaphoreType.DMA((2, n)),
            pltpu.SemaphoreType.DMA((2, n)),
            pltpu.SemaphoreType.DMA((count,)),
            pltpu.SemaphoreType.DMA((count,)),
            pltpu.SemaphoreType.DMA((2,)),
        ],
        compiler_params=pltpu.CompilerParams(collective_id=0, has_side_effects=True),
    )(gen, shift, *arrays)
    if not whole:
        all_gen = jnp.transpose(all_gen, (1, 0, 2)).reshape(2, n * width)
        all_shift = jnp.transpose(all_shift, (1, 2, 0, 3)).reshape(2, LOCAL_REPLICAS, n * width)
    return all_gen, all_shift, mate


def mix_kernel(gen, shift, *refs):
    own, mate = refs[:8], refs[8:16]
    codes, scale, net, even, odd, base, mixed, args = refs[16:]
    load_own, load_mate = own[-1], mate[-1]
    step = pl.program_id(0)
    last = pl.num_programs(0) - 1
    width = gen.shape[1]
    rows = load_own.shape[0]
    tile = 16
    group = 4
    span = group * POINTS

    @pl.when(step == 0)
    def _():
        mixed[...] = jnp.zeros_like(mixed)
        odd[...] = jnp.zeros_like(odd)

    def draw(into, t, r, place):
        offsets = shift[t, pl.ds(r, 1), :]
        for part in range(POINTS // tile):
            index = (base[t, part * tile : (part + 1) * tile, :] + offsets) & (LATTICE - 1)
            x = index.astype(jnp.float32) * (2.0 / LATTICE) + (1.0 / LATTICE - 1.0)
            power = jnp.log((1.0 - x) * (1.0 + x)) * LOG_SCALE - 1.0
            ratio = power * NORMAL_TERMS[-1] + NORMAL_TERMS[-2]
            for term in NORMAL_TERMS[-3::-1]:
                ratio = ratio * power + term
            into[pl.ds(pl.multiple_of(place + part * tile, tile), tile), :] = (ratio * x).astype(jnp.bfloat16)

    def advance(into, source):
        if into is not None:
            points = lax.broadcasted_iota(jnp.int32, (POINTS, width), 0)
            for t in range(2):
                base[t] = points * gen[t : t + 1, :]

        def some(m, carry):
            start = pl.multiple_of(m * span, span)
            left = source[pl.ds(start, span), :]
            for half, load in enumerate((load_own, load_mate)):
                mixed[half, pl.ds(start, span), :] += lax.dot_general(
                    left, load[...], (((1,), (1,)), ((), ())), preferred_element_type=jnp.float32
                )
            if into is not None:
                t = lax.div(m, LOCAL // span)
                first = lax.rem(m, LOCAL // span) * group
                for r in range(group):
                    draw(into, t, first + r, start + r * POINTS)
            return carry

        lax.fori_loop(0, 2 * LOCAL // span, some, 0)

    @pl.when((step < last) & (lax.rem(step, 2) == 0))
    def _():
        advance(even, odd)

    @pl.when((step < last) & (lax.rem(step, 2) == 1))
    def _():
        advance(odd, even)

    @pl.when(step == last)
    def _():
        advance(None, odd)
        picks = []
        members = []
        n_rows = net.shape[0] * NSET_DEV
        for block, slot, owner, _, _, weight, _, _ in (own, mate):
            weights = jnp.concatenate([weight[...]] * (rows // BLOCK), axis=0)
            home = lax.shift_right_logical(lax.broadcasted_iota(jnp.int32, weights.shape, 0), 3)
            pick = jnp.where(home == block[...].reshape(1, -1), weights, 0.0)
            parts = []
            for _ in range(3):
                part = pick.astype(jnp.bfloat16)
                parts.append(part)
                pick = pick - part.astype(jnp.float32)
            picks.append(parts)
            sets = owner[...] * NSET_DEV + slot[...].reshape(1, -1)
            members.append(
                jnp.where(lax.broadcasted_iota(jnp.int32, (n_rows, sets.shape[1]), 0) == sets, 1.0, 0.0).astype(jnp.bfloat16)
            )
        chunk = CHUNK
        largest = 0.0
        sums_of = []
        for m in range(LOCAL // chunk):
            low = slice(m * chunk, (m + 1) * chunk)
            high = slice(LOCAL + m * chunk, LOCAL + (m + 1) * chunk)
            totals = [0.0, 0.0]
            sums = 0.0
            for half, (_, _, _, notional, strike, _, proj, _) in enumerate((own, mate)):
                first = mixed[half, low, :]
                second = mixed[half, high, :]
                state = [
                    first.astype(jnp.bfloat16),
                    (keep_share * first + new_share * second).astype(jnp.bfloat16),
                ]
                for t in range(2):
                    totals[t] = totals[t] + jnp.dot(state[t], proj[...], preferred_element_type=jnp.float32)
                driver = 0.0
                for part in picks[half]:
                    driver = driver + jnp.dot(state[1], part, preferred_element_type=jnp.float32)
                value = (notional[...].reshape(1, -1) * (jnp.exp(drift_rate * driver) - strike[...].reshape(1, -1))).astype(jnp.bfloat16)
                sums = sums + lax.dot_general(
                    members[half], value, (((1,), (1,)), ((), ())), preferred_element_type=jnp.float32
                )
            for t in range(2):
                args[t, low, :] = totals[t]
                largest = jnp.maximum(largest, jnp.max(jnp.abs(totals[t])))
            sums_of.append(sums.reshape(net.shape[0], NSET_DEV, chunk))
        net[...] = jnp.concatenate(sums_of, axis=1).astype(jnp.bfloat16)
        unit = jnp.full(scale.shape, jnp.maximum(largest, 1e-30) * (1.0 / CODES), jnp.float32)
        scale[...] = unit
        inverse = 1.0 / unit[:1, :1]
        span = codes.shape[1] // 2
        for pair in range(codes.shape[0]):
            piece = jnp.concatenate([args[t, pair * span : (pair + 1) * span, :] for t in range(2)], axis=0)
            codes[pair] = encode(piece * inverse)


def mix(gen, shift, own, mate, n):
    rows, factors = own[-1].shape
    width = 512
    basis = own[-2].shape[1]
    pairs = n // SHARE
    codes_shape = (pairs, 2 * LOCAL // pairs, basis)
    net_shape = (n, NSET_DEV * LOCAL // CHUNK, CHUNK)
    steps = factors // width
    assert steps % 2 == 0
    loads = pl.BlockSpec((rows, width), lambda j: (0, jnp.maximum(j - 1, 0)))
    side = [pl.BlockSpec(array.shape, functools.partial(lambda ndim, j: (0,) * ndim, array.ndim)) for array in own[:-1]] + [loads]
    return pl.pallas_call(
        mix_kernel,
        grid=(steps + 1,),
        out_shape=(
            jax.ShapeDtypeStruct(codes_shape, jnp.int16),
            jax.ShapeDtypeStruct((8, 128), jnp.float32),
            jax.ShapeDtypeStruct(net_shape, jnp.bfloat16),
        ),
        in_specs=[
            pl.BlockSpec((2, width), lambda j: (0, jnp.minimum(j, steps - 1))),
            pl.BlockSpec((2, LOCAL_REPLICAS, width), lambda j: (0, 0, jnp.minimum(j, steps - 1))),
        ]
        + side
        + side,
        out_specs=(
            pl.BlockSpec(codes_shape, lambda j: (0, 0, 0)),
            pl.BlockSpec((8, 128), lambda j: (0, 0)),
            pl.BlockSpec(net_shape, lambda j: (0, 0, 0)),
        ),
        scratch_shapes=[
            pltpu.VMEM((2 * LOCAL, width), jnp.bfloat16),
            pltpu.VMEM((2 * LOCAL, width), jnp.bfloat16),
            pltpu.VMEM((2, POINTS, width), jnp.int32),
            pltpu.VMEM((2, 2 * LOCAL, rows), jnp.float32),
            pltpu.VMEM((2, LOCAL, basis), jnp.float32),
        ],
        compiler_params=pltpu.CompilerParams(vmem_limit_bytes=VMEM_LIMIT),
    )(gen, shift, *own, *mate)


def reduce_kernel(n, codes, scale, bias, net, phi, net_out, codes_in, scales_in, arg_sends, arg_recvs, scale_sends, scale_recvs, net_sends, net_recvs, phi_sends, phi_recvs, mate_sends, mate_recvs, own):
    me = lax.axis_index("fac")
    core = lax.rem(me, SHARE)
    pair = lax.div(me, SHARE)
    mate = me + 1 - 2 * core
    pairs = n // SHARE
    greet(me, n)

    arg_copies = []
    for step in range(1, pairs):
        other = lax.rem(pair + step, pairs)
        peer = SHARE * other + core
        arg_copies.append(remote(scale, scales_in.at[pair], scale_sends.at[step], scale_recvs.at[step], peer))
        arg_copies.append(remote(codes.at[other], codes_in.at[pair], arg_sends.at[step], arg_recvs.at[step], peer))
    net_copies = []
    for step in range(1, n):
        peer = lax.rem(me + step, n)
        net_copies.append(remote(net.at[peer], net_out.at[me], net_sends.at[step], net_recvs.at[step], peer))
    for copy in arg_copies + net_copies:
        copy.start()
    keep = pltpu.make_async_copy(net.at[me], net_out.at[me], own)
    keep.start()
    total = decode(codes[pair]) * scale[:1, :1] + bias[...]
    for copy in arg_copies:
        copy.wait_recv()
    for step in range(1, pairs):
        other = lax.rem(pair + step, pairs)
        total = total + decode(codes_in[other]) * scales_in[other][:1, :1]
    phi[me] = encode(jnp.tanh(total) * CODES)
    phi_copies = []
    for step in range(1, pairs):
        peer = SHARE * lax.rem(pair + step, pairs) + core
        phi_copies.append(remote(phi.at[me], phi.at[me], phi_sends.at[step], phi_recvs.at[step], peer))
    mate_copies = [remote(phi.at[me], phi.at[me], mate_sends.at[0], mate_recvs.at[0], mate)]
    for copy in phi_copies + mate_copies:
        copy.start()
    for step in range(1, pairs):
        phi_copies[step - 1].wait_recv()
        there = SHARE * lax.rem(pair - step + pairs, pairs) + core
        forward = remote(phi.at[there], phi.at[there], mate_sends.at[step], mate_recvs.at[step], mate)
        forward.start()
        mate_copies.append(forward)
    keep.wait()
    for copy in net_copies:
        copy.wait_recv()
    for copy in mate_copies:
        copy.wait_recv()
    for copy in arg_copies + net_copies + phi_copies + mate_copies:
        copy.wait_send()


def reduce(codes, scale, bias, net):
    n = net.shape[0]
    pairs = n // SHARE
    vmem = pl.BlockSpec(memory_space=pltpu.VMEM)
    sems = [pltpu.SemaphoreType.DMA((k,)) for k in (pairs, pairs, pairs, pairs, n, n, pairs, pairs, pairs, pairs)]
    return pl.pallas_call(
        functools.partial(reduce_kernel, n),
        out_shape=(
            jax.ShapeDtypeStruct((n,) + codes.shape[1:], codes.dtype),
            jax.ShapeDtypeStruct(net.shape, net.dtype),
        ),
        in_specs=[vmem] * 4,
        out_specs=(vmem, vmem),
        scratch_shapes=[pltpu.VMEM(codes.shape, codes.dtype), pltpu.VMEM((pairs, 8, 128), jnp.float32)]
        + sems
        + [pltpu.SemaphoreType.DMA],
        compiler_params=pltpu.CompilerParams(collective_id=1, has_side_effects=True, vmem_limit_bytes=VMEM_LIMIT),
    )(codes, scale, bias, net)


def regress_kernel(phi_codes, net, fitted, exposure, phi):
    n = net.shape[0]
    basis = phi.shape[2]
    span = phi_codes.shape[1] // 2
    for index in range(n):
        piece = decode(phi_codes[index]) * (1.0 / CODES)
        start = (index % SHARE) * LOCAL + (index // SHARE) * span
        for t in range(2):
            phi[t, start : start + span, :] = piece[t * span : (t + 1) * span]
    parts = []
    for core in range(SHARE):
        side = net[core].astype(jnp.float32)
        for pair in range(1, n // SHARE):
            side = side + net[SHARE * pair + core].astype(jnp.float32)
        parts += [side[m * NSET_DEV : (m + 1) * NSET_DEV] for m in range(LOCAL // CHUNK)]
    netting = jnp.concatenate(parts, axis=1)
    eye = jnp.where(
        lax.broadcasted_iota(jnp.int32, (basis, basis), 0) == lax.broadcasted_iota(jnp.int32, (basis, basis), 1),
        1.0,
        0.0,
    )
    dot = functools.partial(jnp.dot, precision=HIGH, preferred_element_type=jnp.float32)
    grams = []
    rhs = []
    for t in range(2):
        basis_values = phi[t]
        grams.append(
            lax.dot_general(
                basis_values, basis_values, (((0,), (0,)), ((), ())), precision=HIGH, preferred_element_type=jnp.float32
            )
            * (1.0 / SCENARIOS)
            + ridge_term * eye
        )
        rhs.append(dot(netting, basis_values) * (1.0 / SCENARIOS))
    least, most = ridge_term, basis + ridge_term
    spread = (most - least) / (most + least)
    inverses = [eye * (2.0 / (most + least))] * 2
    for _ in range(INVERSE_STEPS):
        scale = 2.0 / (2.0 - spread * spread)
        spread = spread * spread / (2.0 - spread * spread)
        products = [dot(grams[t], inverses[t]) for t in range(2)]
        inverses = [scale * (2.0 * inverses[t] - dot(inverses[t], products[t])) for t in range(2)]
    for t in range(2):
        coeffs = dot(rhs[t], inverses[t])
        coeffs = coeffs + dot(rhs[t] - dot(coeffs, grams[t]), inverses[t])
        values = lax.dot_general(
            coeffs, phi[t], (((1,), (1,)), ((), ())), precision=HIGH, preferred_element_type=jnp.float32
        )
        fitted[t] = values
        exposure[:, t : t + 1] = jnp.sum(jnp.maximum(values, 0.0), axis=1, keepdims=True) * (1.0 / SCENARIOS)


def regress(phi, net):
    vmem = pl.BlockSpec(memory_space=pltpu.VMEM)
    return pl.pallas_call(
        regress_kernel,
        out_shape=(
            jax.ShapeDtypeStruct((2, NSET_DEV, SCENARIOS), jnp.float32),
            jax.ShapeDtypeStruct((NSET_DEV, 2), jnp.float32),
        ),
        in_specs=[vmem] * 2,
        out_specs=(vmem, vmem),
        scratch_shapes=[pltpu.VMEM((2, SCENARIOS, phi.shape[2]), jnp.float32)],
        compiler_params=pltpu.CompilerParams(vmem_limit_bytes=VMEM_LIMIT),
    )(phi, net)


def local(
    lattice_gen,
    lattice_shift,
    loading,
    basis_proj,
    basis_bias,
    trade_block,
    trade_weights,
    trade_notional,
    trade_strike,
    trade_owner,
    trade_slot,
):
    n = lax.axis_size("fac")
    own = [
        trade_block,
        trade_slot,
        trade_owner.reshape(1, -1),
        trade_notional,
        trade_strike,
        trade_weights.T,
        basis_proj,
        loading,
    ]
    gen, shift, mate = share(lattice_gen, lattice_shift, own, n)
    codes, scale, net = mix(gen, shift, own, mate, n)
    phi, net = reduce(codes, scale, basis_bias[None, :], net)
    return regress(phi, net)


def solution(mesh):
    return jax.shard_map(
        local,
        mesh=mesh,
        in_specs=(
            P(None, "fac"),
            P(None, "grp", "fac"),
            P("fac", None),
            P("fac", None),
            P(),
            P(("grp", "fac")),
            P(("grp", "fac"), None),
            P(("grp", "fac")),
            P(("grp", "fac")),
            P(("grp", "fac"), None),
            P(("grp", "fac")),
        ),
        out_specs=(P(None, "fac", "grp"), P("fac", "grp")),
        check_vma=False,
    )
```

```python
import functools
import math

import jax
import jax.numpy as jnp
from jax import lax
from jax.experimental import pallas as pl
from jax.experimental.pallas import tpu as pltpu
from jax.sharding import PartitionSpec as P

BLOCK = 8
LATTICE = 65536
REPLICAS = 16
POINTS = 64
NSET_DEV = 24
SHARE = 2
SCENARIOS = REPLICAS * POINTS
LOCAL = SCENARIOS // SHARE
LOCAL_REPLICAS = REPLICAS // SHARE

drift_rate = 0.25
ridge_term = 0.01
keep_share = 0.8
new_share = 0.6

VMEM_LIMIT = 56 * 1024 * 1024
HIGH = lax.Precision.HIGHEST
MESH = pl.DeviceIdType.MESH

LOG_SCALE = -2.0 / (15.001 * math.log(2.0))
NORMAL_TERMS = (
    3.00101966e00,
    1.55010142e00,
    -2.74155082e-01,
    3.36067480e-02,
    4.31695681e-02,
    -5.08279578e-02,
    3.10899462e-02,
    -1.21453725e-03,
    -1.43043690e-02,
    4.24694167e-03,
    2.40633730e-03,
)

INVERSE_STEPS = 10

CODES = 32767.0
CHUNK = 128


def encode(values):
    return jnp.round(values).astype(jnp.int32).astype(jnp.int16)


def decode(codes):
    return codes.astype(jnp.int32).astype(jnp.float32)


def greet(me, n):
    barrier = pltpu.get_barrier_semaphore()
    for step in range(1, n):
        pl.semaphore_signal(
            barrier, inc=1, device_id={"fac": lax.rem(me + step, n)}, device_id_type=MESH
        )
    pl.semaphore_wait(barrier, n - 1)


def remote(src, dst, send, recv, peer):
    return pltpu.make_async_remote_copy(
        src_ref=src,
        dst_ref=dst,
        send_sem=send,
        recv_sem=recv,
        device_id={"fac": peer},
        device_id_type=MESH,
    )


def share_kernel(n, *refs):
    count = (len(refs) - 5) // 2
    gen, shift, *mine = refs[:count]
    gen_out, shift_out, *theirs = refs[count : 2 * count]
    sends, recvs, mate_sends, mate_recvs, own = refs[2 * count :]
    me = lax.axis_index("fac")
    core = lax.rem(me, SHARE)
    mate = me + 1 - 2 * core
    width = gen.shape[1]
    if len(gen_out.shape) == 2:
        columns = pl.ds(pl.multiple_of(me * width, 128), width)
        gen_to, shift_to = gen_out.at[:, columns], shift_out.at[:, :, columns]
    else:
        gen_to, shift_to = gen_out.at[me], shift_out.at[me]

    def replicas(side):
        return shift.at[:, pl.ds(pl.multiple_of(side * LOCAL_REPLICAS, LOCAL_REPLICAS), LOCAL_REPLICAS), :]

    greet(me, n)
    copies = []
    for step in range(1, n):
        peer = lax.rem(me + step, n)
        copies.append(remote(gen, gen_to, sends.at[0, step], recvs.at[0, step], peer))
        copies.append(remote(replicas(lax.rem(peer, SHARE)), shift_to, sends.at[1, step], recvs.at[1, step], peer))
    for index, (src, dst) in enumerate(zip(mine, theirs)):
        copies.append(remote(src, dst, mate_sends.at[index], mate_recvs.at[index], mate))
    for copy in copies:
        copy.start()
    keeps = [
        pltpu.make_async_copy(gen, gen_to, own.at[0]),
        pltpu.make_async_copy(replicas(core), shift_to, own.at[1]),
    ]
    for keep in keeps:
        keep.start()
    for copy in keeps + copies:
        copy.wait()


def share(gen, shift, arrays, n):
    hbm = pl.BlockSpec(memory_space=pl.ANY)
    count = len(arrays)
    width = gen.shape[1]
    whole = width % 128 == 0
    if whole:
        shapes = [(2, n * width), (2, LOCAL_REPLICAS, n * width)]
    else:
        shapes = [(n, 2, width), (n, 2, LOCAL_REPLICAS, width)]
    all_gen, all_shift, *mate = pl.pallas_call(
        functools.partial(share_kernel, n),
        out_shape=[jax.ShapeDtypeStruct(shape, gen.dtype) for shape in shapes]
        + [jax.ShapeDtypeStruct(array.shape, array.dtype) for array in arrays],
        in_specs=[hbm] * (count + 2),
        out_specs=[hbm] * (count + 2),
        scratch_shapes=[
            pltpu.SemaphoreType.DMA((2, n)),
            pltpu.SemaphoreType.DMA((2, n)),
            pltpu.SemaphoreType.DMA((count,)),
            pltpu.SemaphoreType.DMA((count,)),
            pltpu.SemaphoreType.DMA((2,)),
        ],
        compiler_params=pltpu.CompilerParams(collective_id=0, has_side_effects=True),
    )(gen, shift, *arrays)
    if not whole:
        all_gen = jnp.transpose(all_gen, (1, 0, 2)).reshape(2, n * width)
        all_shift = jnp.transpose(all_shift, (1, 2, 0, 3)).reshape(2, LOCAL_REPLICAS, n * width)
    return all_gen, all_shift, mate


def mix_kernel(gen, shift, *refs):
    own, mate = refs[:8], refs[8:16]
    codes, scale, net, even, odd, base, mixed, args = refs[16:]
    load_own, load_mate = own[-1], mate[-1]
    step = pl.program_id(0)
    last = pl.num_programs(0) - 1
    width = gen.shape[1]
    rows = load_own.shape[0]
    tile = 16
    group = 4
    span = group * POINTS

    @pl.when(step == 0)
    def _():
        mixed[...] = jnp.zeros_like(mixed)
        odd[...] = jnp.zeros_like(odd)

    def draw(into, t, r, place):
        offsets = shift[t, pl.ds(r, 1), :]
        for part in range(POINTS // tile):
            index = (base[t, part * tile : (part + 1) * tile, :] + offsets) & (LATTICE - 1)
            x = index.astype(jnp.float32) * (2.0 / LATTICE) + (1.0 / LATTICE - 1.0)
            power = jnp.log((1.0 - x) * (1.0 + x)) * LOG_SCALE - 1.0
            ratio = power * NORMAL_TERMS[-1] + NORMAL_TERMS[-2]
            for term in NORMAL_TERMS[-3::-1]:
                ratio = ratio * power + term
            into[pl.ds(pl.multiple_of(place + part * tile, tile), tile), :] = (ratio * x).astype(jnp.bfloat16)

    def advance(into, source):
        if into is not None:
            points = lax.broadcasted_iota(jnp.int32, (POINTS, width), 0)
            for t in range(2):
                base[t] = points * gen[t : t + 1, :]

        def some(m, carry):
            start = pl.multiple_of(m * span, span)
            left = source[pl.ds(start, span), :]
            for half, load in enumerate((load_own, load_mate)):
                mixed[half, pl.ds(start, span), :] += lax.dot_general(
                    left, load[...], (((1,), (1,)), ((), ())), preferred_element_type=jnp.float32
                )
            if into is not None:
                t = lax.div(m, LOCAL // span)
                first = lax.rem(m, LOCAL // span) * group
                for r in range(group):
                    draw(into, t, first + r, start + r * POINTS)
            return carry

        lax.fori_loop(0, 2 * LOCAL // span, some, 0)

    @pl.when((step < last) & (lax.rem(step, 2) == 0))
    def _():
        advance(even, odd)

    @pl.when((step < last) & (lax.rem(step, 2) == 1))
    def _():
        advance(odd, even)

    @pl.when(step == last)
    def _():
        advance(None, odd)
        picks = []
        members = []
        n_rows = net.shape[0] * NSET_DEV
        for block, slot, owner, _, _, weight, _, _ in (own, mate):
            weights = jnp.concatenate([weight[...]] * (rows // BLOCK), axis=0)
            home = lax.shift_right_logical(lax.broadcasted_iota(jnp.int32, weights.shape, 0), 3)
            pick = jnp.where(home == block[...].reshape(1, -1), weights, 0.0)
            parts = []
            for _ in range(3):
                part = pick.astype(jnp.bfloat16)
                parts.append(part)
                pick = pick - part.astype(jnp.float32)
            picks.append(parts)
            sets = owner[...] * NSET_DEV + slot[...].reshape(1, -1)
            members.append(
                jnp.where(lax.broadcasted_iota(jnp.int32, (n_rows, sets.shape[1]), 0) == sets, 1.0, 0.0).astype(jnp.bfloat16)
            )
        chunk = CHUNK
        largest = 0.0
        sums_of = []
        for m in range(LOCAL // chunk):
            low = slice(m * chunk, (m + 1) * chunk)
            high = slice(LOCAL + m * chunk, LOCAL + (m + 1) * chunk)
            totals = [0.0, 0.0]
            sums = 0.0
            for half, (_, _, _, notional, strike, _, proj, _) in enumerate((own, mate)):
                first = mixed[half, low, :]
                second = mixed[half, high, :]
                state = [
                    first.astype(jnp.bfloat16),
                    (keep_share * first + new_share * second).astype(jnp.bfloat16),
                ]
                for t in range(2):
                    totals[t] = totals[t] + jnp.dot(state[t], proj[...], preferred_element_type=jnp.float32)
                driver = 0.0
                for part in picks[half]:
                    driver = driver + jnp.dot(state[1], part, preferred_element_type=jnp.float32)
                value = (notional[...].reshape(1, -1) * (jnp.exp(drift_rate * driver) - strike[...].reshape(1, -1))).astype(jnp.bfloat16)
                sums = sums + lax.dot_general(
                    members[half], value, (((1,), (1,)), ((), ())), preferred_element_type=jnp.float32
                )
            for t in range(2):
                args[t, low, :] = totals[t]
                largest = jnp.maximum(largest, jnp.max(jnp.abs(totals[t])))
            sums_of.append(sums.reshape(net.shape[0], NSET_DEV, chunk))
        net[...] = jnp.concatenate(sums_of, axis=1).astype(jnp.bfloat16)
        unit = jnp.full(scale.shape, jnp.maximum(largest, 1e-30) * (1.0 / CODES), jnp.float32)
        scale[...] = unit
        inverse = 1.0 / unit[:1, :1]
        span = codes.shape[1] // 2
        for pair in range(codes.shape[0]):
            piece = jnp.concatenate([args[t, pair * span : (pair + 1) * span, :] for t in range(2)], axis=0)
            codes[pair] = encode(piece * inverse)


def mix(gen, shift, own, mate, n):
    rows, factors = own[-1].shape
    width = 512
    basis = own[-2].shape[1]
    pairs = n // SHARE
    codes_shape = (pairs, 2 * LOCAL // pairs, basis)
    net_shape = (n, NSET_DEV * LOCAL // CHUNK, CHUNK)
    steps = factors // width
    assert steps % 2 == 0
    loads = pl.BlockSpec((rows, width), lambda j: (0, jnp.maximum(j - 1, 0)))
    side = [pl.BlockSpec(array.shape, functools.partial(lambda ndim, j: (0,) * ndim, array.ndim)) for array in own[:-1]] + [loads]
    return pl.pallas_call(
        mix_kernel,
        grid=(steps + 1,),
        out_shape=(
            jax.ShapeDtypeStruct(codes_shape, jnp.int16),
            jax.ShapeDtypeStruct((8, 128), jnp.float32),
            jax.ShapeDtypeStruct(net_shape, jnp.bfloat16),
        ),
        in_specs=[
            pl.BlockSpec((2, width), lambda j: (0, jnp.minimum(j, steps - 1))),
            pl.BlockSpec((2, LOCAL_REPLICAS, width), lambda j: (0, 0, jnp.minimum(j, steps - 1))),
        ]
        + side
        + side,
        out_specs=(
            pl.BlockSpec(codes_shape, lambda j: (0, 0, 0)),
            pl.BlockSpec((8, 128), lambda j: (0, 0)),
            pl.BlockSpec(net_shape, lambda j: (0, 0, 0)),
        ),
        scratch_shapes=[
            pltpu.VMEM((2 * LOCAL, width), jnp.bfloat16),
            pltpu.VMEM((2 * LOCAL, width), jnp.bfloat16),
            pltpu.VMEM((2, POINTS, width), jnp.int32),
            pltpu.VMEM((2, 2 * LOCAL, rows), jnp.float32),
            pltpu.VMEM((2, LOCAL, basis), jnp.float32),
        ],
        compiler_params=pltpu.CompilerParams(vmem_limit_bytes=VMEM_LIMIT),
    )(gen, shift, *own, *mate)


def reduce_kernel(n, codes, scale, bias, net, phi, net_out, codes_in, scales_in, arg_sends, arg_recvs, scale_sends, scale_recvs, net_sends, net_recvs, phi_sends, phi_recvs, mate_sends, mate_recvs, own):
    me = lax.axis_index("fac")
    core = lax.rem(me, SHARE)
    pair = lax.div(me, SHARE)
    mate = me + 1 - 2 * core
    pairs = n // SHARE
    greet(me, n)

    arg_copies = []
    for step in range(1, pairs):
        other = lax.rem(pair + step, pairs)
        peer = SHARE * other + core
        arg_copies.append(remote(scale, scales_in.at[pair], scale_sends.at[step], scale_recvs.at[step], peer))
        arg_copies.append(remote(codes.at[other], codes_in.at[pair], arg_sends.at[step], arg_recvs.at[step], peer))
    net_copies = []
    for step in range(1, n):
        peer = lax.rem(me + step, n)
        net_copies.append(remote(net.at[peer], net_out.at[me], net_sends.at[step], net_recvs.at[step], peer))
    for copy in arg_copies:
        copy.start()
    keep = pltpu.make_async_copy(net.at[me], net_out.at[me], own)
    keep.start()
    total = decode(codes[pair]) * scale[:1, :1] + bias[...]
    for copy in arg_copies:
        copy.wait_recv()
    for copy in net_copies:
        copy.start()
    for step in range(1, pairs):
        other = lax.rem(pair + step, pairs)
        total = total + decode(codes_in[other]) * scales_in[other][:1, :1]
    phi[me] = encode(jnp.tanh(total) * CODES)
    phi_copies = []
    for step in range(1, pairs):
        peer = SHARE * lax.rem(pair + step, pairs) + core
        phi_copies.append(remote(phi.at[me], phi.at[me], phi_sends.at[step], phi_recvs.at[step], peer))
    mate_copies = [remote(phi.at[me], phi.at[me], mate_sends.at[0], mate_recvs.at[0], mate)]
    for copy in phi_copies + mate_copies:
        copy.start()
    for step in range(1, pairs):
        phi_copies[step - 1].wait_recv()
        there = SHARE * lax.rem(pair - step + pairs, pairs) + core
        forward = remote(phi.at[there], phi.at[there], mate_sends.at[step], mate_recvs.at[step], mate)
        forward.start()
        mate_copies.append(forward)
    keep.wait()
    for copy in net_copies:
        copy.wait_recv()
    for copy in mate_copies:
        copy.wait_recv()
    for copy in arg_copies + net_copies + phi_copies + mate_copies:
        copy.wait_send()


def reduce(codes, scale, bias, net):
    n = net.shape[0]
    pairs = n // SHARE
    vmem = pl.BlockSpec(memory_space=pltpu.VMEM)
    sems = [pltpu.SemaphoreType.DMA((k,)) for k in (pairs, pairs, pairs, pairs, n, n, pairs, pairs, pairs, pairs)]
    return pl.pallas_call(
        functools.partial(reduce_kernel, n),
        out_shape=(
            jax.ShapeDtypeStruct((n,) + codes.shape[1:], codes.dtype),
            jax.ShapeDtypeStruct(net.shape, net.dtype),
        ),
        in_specs=[vmem] * 4,
        out_specs=(vmem, vmem),
        scratch_shapes=[pltpu.VMEM(codes.shape, codes.dtype), pltpu.VMEM((pairs, 8, 128), jnp.float32)]
        + sems
        + [pltpu.SemaphoreType.DMA],
        compiler_params=pltpu.CompilerParams(collective_id=1, has_side_effects=True, vmem_limit_bytes=VMEM_LIMIT),
    )(codes, scale, bias, net)


def regress_kernel(phi_codes, net, fitted, exposure, phi):
    n = net.shape[0]
    basis = phi.shape[2]
    span = phi_codes.shape[1] // 2
    for index in range(n):
        piece = decode(phi_codes[index]) * (1.0 / CODES)
        start = (index % SHARE) * LOCAL + (index // SHARE) * span
        for t in range(2):
            phi[t, start : start + span, :] = piece[t * span : (t + 1) * span]
    parts = []
    for core in range(SHARE):
        side = net[core].astype(jnp.float32)
        for pair in range(1, n // SHARE):
            side = side + net[SHARE * pair + core].astype(jnp.float32)
        parts += [side[m * NSET_DEV : (m + 1) * NSET_DEV] for m in range(LOCAL // CHUNK)]
    netting = jnp.concatenate(parts, axis=1)
    eye = jnp.where(
        lax.broadcasted_iota(jnp.int32, (basis, basis), 0) == lax.broadcasted_iota(jnp.int32, (basis, basis), 1),
        1.0,
        0.0,
    )
    dot = functools.partial(jnp.dot, precision=HIGH, preferred_element_type=jnp.float32)
    grams = []
    rhs = []
    for t in range(2):
        basis_values = phi[t]
        grams.append(
            lax.dot_general(
                basis_values, basis_values, (((0,), (0,)), ((), ())), precision=HIGH, preferred_element_type=jnp.float32
            )
            * (1.0 / SCENARIOS)
            + ridge_term * eye
        )
        rhs.append(dot(netting, basis_values) * (1.0 / SCENARIOS))
    least, most = ridge_term, basis + ridge_term
    spread = (most - least) / (most + least)
    inverses = [eye * (2.0 / (most + least))] * 2
    for _ in range(INVERSE_STEPS):
        scale = 2.0 / (2.0 - spread * spread)
        spread = spread * spread / (2.0 - spread * spread)
        products = [dot(grams[t], inverses[t]) for t in range(2)]
        inverses = [scale * (2.0 * inverses[t] - dot(inverses[t], products[t])) for t in range(2)]
    for t in range(2):
        coeffs = dot(rhs[t], inverses[t])
        coeffs = coeffs + dot(rhs[t] - dot(coeffs, grams[t]), inverses[t])
        values = lax.dot_general(
            coeffs, phi[t], (((1,), (1,)), ((), ())), precision=HIGH, preferred_element_type=jnp.float32
        )
        fitted[t] = values
        exposure[:, t : t + 1] = jnp.sum(jnp.maximum(values, 0.0), axis=1, keepdims=True) * (1.0 / SCENARIOS)


def regress(phi, net):
    vmem = pl.BlockSpec(memory_space=pltpu.VMEM)
    return pl.pallas_call(
        regress_kernel,
        out_shape=(
            jax.ShapeDtypeStruct((2, NSET_DEV, SCENARIOS), jnp.float32),
            jax.ShapeDtypeStruct((NSET_DEV, 2), jnp.float32),
        ),
        in_specs=[vmem] * 2,
        out_specs=(vmem, vmem),
        scratch_shapes=[pltpu.VMEM((2, SCENARIOS, phi.shape[2]), jnp.float32)],
        compiler_params=pltpu.CompilerParams(vmem_limit_bytes=VMEM_LIMIT),
    )(phi, net)


def local(
    lattice_gen,
    lattice_shift,
    loading,
    basis_proj,
    basis_bias,
    trade_block,
    trade_weights,
    trade_notional,
    trade_strike,
    trade_owner,
    trade_slot,
):
    n = lax.axis_size("fac")
    own = [
        trade_block,
        trade_slot,
        trade_owner.reshape(1, -1),
        trade_notional,
        trade_strike,
        trade_weights.T,
        basis_proj,
        loading,
    ]
    gen, shift, mate = share(lattice_gen, lattice_shift, own, n)
    codes, scale, net = mix(gen, shift, own, mate, n)
    phi, net = reduce(codes, scale, basis_bias[None, :], net)
    return regress(phi, net)


def solution(mesh):
    return jax.shard_map(
        local,
        mesh=mesh,
        in_specs=(
            P(None, "fac"),
            P(None, "grp", "fac"),
            P("fac", None),
            P("fac", None),
            P(),
            P(("grp", "fac")),
            P(("grp", "fac"), None),
            P(("grp", "fac")),
            P(("grp", "fac")),
            P(("grp", "fac"), None),
            P(("grp", "fac")),
        ),
        out_specs=(P(None, "fac", "grp"), P("fac", "grp")),
        check_vma=False,
    )
```
